32 devices in a mesh: grp: 2 (over y), fit: 8 (over z, core), occ: 2 (over x), sub: 1.
Axes of the slice: x: 2, y: 2, z: 4, core: 2. Of those that a mesh axis runs over, the one named last changes fastest.
Arguments:
- tiles: bfloat16 [192, 3, 64, 8192], P(('grp', 'fit'), None, None, ('occ', 'sub')), parts along dimension 0, may hold values from -0.015625 to 0.015625
- metric: bfloat16 [192, 64, 64], P(('grp', 'fit')), parts along dimension 0, may hold values from -1 to 2, as said below
- owners: int32 [192, 3], P(('grp', 'fit')), parts along dimension 0, may hold values from 0 to 7, all different within a row; in each aligned block of 12 rows (0 to 11, 12 to 23, ...) at most 9 rows name the same one
Outputs:
- exchange_blocks: bfloat16 [16, 128, 128], P(('grp', 'fit'), ('occ', 'sub')), parts along dimension 0
The draws below stay inside these ranges and needn't reach their ends.
There are 2 independent parts, one for each index of `grp`. The reference program is written for one: setup_inputs(seed, part) draws one part's arguments, and reference() takes and returns one part's arrays. A program takes and returns all parts, laid end to end along the dimension named above; each array names one. Nothing has to cross between parts.
Inputs may be any that keep to these rules, and one draw needn't show every extreme that they name: Each row names 3 different owners. Among the 12 rows of one index of fit no owner is named more than 9 times, and in some such block one owner is named exactly 9 times. `metric`: each tile is lower triangular with a positive diagonal of at most 2.
All inputs are finite; a program needn't handle non-finite values.
Results may differ from the reference program's by a relative error of at most 0.0065.
Values may be sent and summed in bfloat16 or wider, within the bound.
A program may use at most 128 MiB of HBM per device.

```python
import math
import jax
import jax.numpy as jnp
import numpy as np
from jax import lax

TP = 64
BLK = 128
NOCC = 64
FT_DEV = 12
PAIRS = 3
F_ALL = 96
CAP = 9
N_FIT = 8


def draw_metric(key, part):
    key = jax.random.fold_in(key, 11)
    first_key, second_key = jax.random.split(key)
    row_ids = jnp.arange(TP)[:, None]
    col_ids = jnp.arange(TP)[None, :]
    below = (col_ids < row_ids).astype(jnp.float32)
    on_diag = (col_ids == row_ids).astype(jnp.float32)
    diag_values = jax.random.uniform(first_key, (F_ALL, TP), jnp.float32, 0.6, 1.4)
    lower_values = jnp.clip(jax.random.normal(second_key, (F_ALL, TP, TP), jnp.float32), -3.0, 3.0) * 0.9 / TP ** 0.5
    full = lower_values * below[None] + diag_values[:, :, None] * on_diag[None]
    return full.astype(jnp.bfloat16)


def level_of(rng, shape, cuts, smallest, high):
    loudness, own = 1.0, jax.random.fold_in(rng, 6)
    for position, shards_of in cuts:
        steps = jnp.exp(jax.random.uniform(jax.random.fold_in(own, position), (shards_of,), jnp.float32, smallest / len(cuts), high / len(cuts)))
        loudness = loudness * jnp.repeat(steps, shape[position] // shards_of).reshape([-1 if axis == position else 1 for axis in range(len(shape))])
    return loudness


def routed_block(stream_key, own, number, rows, count, top, limit, skew):
    order = jax.random.permutation(stream_key, count)
    crowded, common = portions_of(count, rows * top, limit, skew, True), portions_of(count, rows * top, limit, skew, False)
    places = jnp.arange(count)

    def named(sizes, offset_by):
        used = int((sizes > 0).sum())
        fixed = max(1, used // 4)
        passed = fixed + (places - fixed + offset_by * (used - fixed)) % max(1, count - fixed)
        return jnp.zeros((count,), jnp.int32).at[order[jnp.where(places < fixed, places, passed)]].set(jnp.asarray(sizes, jnp.int32))

    sizes = jnp.where(number % 4 == 0, named(crowded, number // 4), named(common, number - number // 4 - 1))
    mixed = jax.random.permutation(jax.random.fold_in(own, 3), count)
    donor, sink = mixed[0:count // 2 * 2:2], mixed[1:count // 2 * 2:2]
    margin = jnp.minimum(sizes[donor] - 1, limit - sizes[sink]) // 2
    margin = jnp.where((donor == order[0]) | (sink == order[0]) | (sizes[sink] == 0), 0, jnp.maximum(margin, 0))
    passed = jax.random.randint(jax.random.fold_in(own, 4), (count // 2,), 0, 1 << 20) % (margin + 1)
    sizes = sizes.at[donor].add(-passed).at[sink].add(passed)
    labels = jnp.searchsorted(jnp.cumsum(sizes), jnp.arange(rows * top), side="right").astype(jnp.int32)
    grid = labels.reshape(top, rows).T
    grid = grid[jax.random.permutation(jax.random.fold_in(own, 1), rows)]
    offset_by = jax.random.randint(jax.random.fold_in(own, 2), (rows, 1), 0, top)
    return jnp.take_along_axis(grid, (jnp.arange(top)[None, :] + offset_by) % top, axis=1)


def portions_of(amount, total, bound, slope, full):
    weights = [(1 << 20) // math.isqrt(grade ** slope) + 1 for grade in range(1, amount + 1)]
    largest = bound if full else min(bound, max(-(-total // amount), total * weights[0] // sum(weights)))
    least = 1 if total - largest >= amount - 1 else 0
    given, spare = [largest] + [least] * (amount - 1), total - largest - least * (amount - 1)
    while spare > 0:
        movable = [i for i in range(1, amount) if given[i] < largest] or [i for i in range(1, amount) if given[i] < bound]
        pool, budget = sum([weights[i] for i in movable]), spare
        for i in movable:
            addition = min(bound - given[i], max(1, budget * weights[i] // pool), spare)
            given[i] = given[i] + addition
            spare = spare - addition
    return np.array(given)


def gaussian(rng, extent, width, most, pieces=(), held_as=jnp.bfloat16):
    result = jax.random.normal(rng, extent, jnp.float32) * width
    if len(pieces) > 0:
        result = level_of(rng, extent, pieces, -0.22, 0.18) * result
    return jnp.clip(result, min=-most, max=most).astype(held_as)


def setup_inputs(seed: int = 0, part: int = 0) -> dict:
    splits = jax.random.split(jax.random.key(seed), 4)
    own_keys = jax.random.split(jax.random.fold_in(splits[3], part), 4)
    tiles = gaussian(own_keys[0], (F_ALL, PAIRS, TP, NOCC * BLK), ((TP * NOCC * FT_DEV * PAIRS) ** -0.5), 0.015625, ((0, 8), (3, 2)))
    metric = draw_metric(jax.random.fold_in(jax.random.fold_in(splits[3], part), 71), part)
    owners_keys = jax.random.split(jax.random.fold_in(own_keys[2], 1), F_ALL // FT_DEV)
    owners_turns = jax.random.permutation(jax.random.fold_in(own_keys[2], 3), F_ALL // FT_DEV)
    owners = jax.vmap(lambda own, number: routed_block(jax.random.fold_in(own_keys[2], 2), own, number, FT_DEV, N_FIT, PAIRS, CAP, 2))(owners_keys, owners_turns).reshape((F_ALL, PAIRS))
    return dict(tiles=tiles, metric=metric, owners=owners)


def reference(tiles, metric, owners):
    owner_ids = jnp.arange(N_FIT, dtype=jnp.int32)

    def step(total, index):
        factor = metric[index].astype(jnp.float32)
        pair_tiles = tiles[index].astype(jnp.float32)
        fitted = jnp.einsum("ab,pbw->paw", factor, pair_tiles).astype(jnp.bfloat16)
        shaped = fitted.astype(jnp.float32).reshape(PAIRS, TP, NOCC, BLK)
        gram_blocks = jnp.einsum("pqia,pqib->pab", shaped, shaped)
        selector = (owners[index][:, None] == owner_ids[None, :]).astype(jnp.float32)
        return total + jnp.einsum("pd,pab->dab", selector, gram_blocks), None

    initial = jnp.zeros((N_FIT, BLK, BLK), jnp.float32)
    total, unused = lax.scan(step, initial, jnp.arange(F_ALL, dtype=jnp.int32))
    return total.astype(jnp.bfloat16)
```

```python
import functools

import jax
import jax.numpy as jnp
from jax import lax
from jax.experimental import pallas as pl
from jax.experimental.pallas import tpu as pltpu
from jax.sharding import PartitionSpec as P

BLK = 128
MESH = pl.DeviceIdType.MESH
OVER_ROWS = (((0,), (0,)), ((), ()))


def each(count, step):
    if count <= 16:
        for k in range(count):
            step(k)
    else:
        lax.fori_loop(0, count, lambda k, carry: (step(k), carry)[1], 0)


def kernel(
    sizes, owners, metric, tiles_hbm, out,
    tiles, acc, send1, recv1, send2, recv2,
    load_sem, send1_sem, recv1_sem, send2_sem, recv2_sem,
):
    fit, occ, sub = sizes
    shards = occ * sub
    tile_rows, pairs, _, width = tiles.shape
    count, rows, _ = send1.shape
    my_fit, my_occ, my_sub = lax.axis_index("fit"), lax.axis_index("occ"), lax.axis_index("sub")

    if sub > 1:
        half = sub // 2
        own_class = lax.rem(my_sub, 2)
        my_slot = (my_fit * occ + my_occ) * half + my_sub // 2
        partner = {"fit": my_fit, "occ": my_occ, "sub": my_sub + 1 - 2 * own_class}

        def place(slot, kind):
            return slot // (occ * half), (slot // half) % occ, (slot % half) * 2 + kind
    else:
        own_class = lax.rem(my_fit, 2)
        my_slot = (my_fit // 2) * occ + my_occ
        partner = {"fit": my_fit + 1 - 2 * own_class, "occ": my_occ, "sub": my_sub}

        def place(slot, kind):
            return (slot // occ) * 2 + kind, slot % occ, 0

    def device_of(slot):
        owner, o, s = place(slot, own_class)
        return {"fit": owner, "occ": o, "sub": s}

    def partial(slot, kind):
        owner, o, s = place(slot, kind)
        return acc[owner, pl.ds(pl.multiple_of((o * sub + s) * rows, rows), rows), :]

    def other(k):
        return lax.rem(my_slot + k, count)

    def load(f):
        return pltpu.make_async_copy(tiles_hbm.at[f], tiles.at[f], load_sem.at[f])

    for f in range(tile_rows):
        load(f).start()

    barrier = pltpu.get_barrier_semaphore()
    pl.semaphore_signal(barrier, inc=1, device_id=partner, device_id_type=MESH)
    each(count - 1, lambda k: pl.semaphore_signal(
        barrier, inc=1, device_id=device_of(other(k + 1)), device_id_type=MESH))

    acc[...] = jnp.zeros_like(acc)
    group = 2 if tile_rows % 2 == 0 else 1

    def work(step, carry):
        members = [step * group + g for g in range(group)]
        for f in members:
            load(f).wait()
        stacked = []
        for f in members:
            for p in range(pairs):
                fitted = jnp.dot(
                    metric[f], tiles[f, p], preferred_element_type=jnp.float32
                ).astype(jnp.bfloat16)
                stacked.append(jnp.concatenate(
                    [fitted[:, c:c + BLK] for c in range(0, width, BLK)], axis=0))
        grams = [
            lax.dot_general(x, x, OVER_ROWS, preferred_element_type=jnp.float32) for x in stacked
        ]
        names = [owners[f, p] for f in members for p in range(pairs)]

        def add(d):
            total = acc[d]
            for name, gram in zip(names, grams):
                total = total + jnp.where(name == d, gram, 0.0)
            acc[d] = total

        for d in range(fit):
            add(d)
        return carry

    lax.fori_loop(0, tile_rows // group, work, 0)

    pl.semaphore_wait(barrier, count)

    def swap(slot):
        return pltpu.make_async_remote_copy(
            src_ref=send1.at[slot], dst_ref=recv1.at[slot],
            send_sem=send1_sem.at[slot], recv_sem=recv1_sem.at[slot],
            device_id=partner, device_id_type=MESH)

    def deliver(slot):
        return pltpu.make_async_remote_copy(
            src_ref=send2.at[slot], dst_ref=recv2.at[my_slot],
            send_sem=send2_sem.at[slot], recv_sem=recv2_sem.at[my_slot],
            device_id=device_of(slot), device_id_type=MESH)

    def arrived(slot):
        return pltpu.make_async_remote_copy(
            src_ref=send2.at[slot], dst_ref=recv2.at[slot],
            send_sem=send2_sem.at[slot], recv_sem=recv2_sem.at[slot],
            device_id=device_of(slot), device_id_type=MESH)

    def give(k):
        slot = other(k + 1)
        send1[slot] = partial(slot, 1 - own_class).astype(jnp.bfloat16)
        swap(slot).start()

    each(count, give)

    def summed(slot):
        swap(slot).wait_recv()
        return partial(slot, own_class) + recv1[slot].astype(jnp.float32)

    def pass_on(k):
        slot = other(k + 1)
        send2[slot] = summed(slot).astype(jnp.bfloat16)
        deliver(slot).start()

    each(count - 1, pass_on)
    total = summed(my_slot)

    def collect(k, total):
        slot = other(count - 1 - k)
        arrived(slot).wait_recv()
        return total + recv2[slot].astype(jnp.float32)

    if count <= 16:
        for k in range(count - 1):
            total = collect(k, total)
    else:
        total = lax.fori_loop(0, count - 1, collect, total)
    out[0] = total.astype(out.dtype)

    each(count, lambda k: swap(other(k + 1)).wait_send())
    each(count - 1, lambda k: deliver(other(k + 1)).wait_send())


def on_device(sizes, tiles, metric, owners):
    fit, occ, sub = sizes
    count = fit * occ * sub // 2
    rows = BLK // (occ * sub)
    tile_rows, pairs, fit_rows, width = tiles.shape
    parts = pltpu.VMEM((count, rows, BLK), jnp.bfloat16)
    return pl.pallas_call(
        functools.partial(kernel, sizes),
        out_shape=jax.ShapeDtypeStruct((1, rows, BLK), jnp.bfloat16),
        in_specs=[
            pl.BlockSpec(memory_space=pltpu.SMEM),
            pl.BlockSpec(memory_space=pltpu.VMEM),
            pl.BlockSpec(memory_space=pl.ANY),
        ],
        out_specs=pl.BlockSpec(memory_space=pltpu.VMEM),
        scratch_shapes=[
            pltpu.VMEM(tiles.shape, jnp.bfloat16),
            pltpu.VMEM((fit, BLK, BLK), jnp.float32),
            parts, parts, parts, parts,
            pltpu.SemaphoreType.DMA((tile_rows,)),
            pltpu.SemaphoreType.DMA((count,)),
            pltpu.SemaphoreType.DMA((count,)),
            pltpu.SemaphoreType.DMA((count,)),
            pltpu.SemaphoreType.DMA((count,)),
        ],
        compiler_params=pltpu.CompilerParams(
            collective_id=0, has_side_effects=True, vmem_limit_bytes=56 << 20
        ),
    )(owners, metric, tiles)


def solution(mesh):
    sizes = tuple(mesh.shape[name] for name in ("fit", "occ", "sub"))
    placed = (
        P(("grp", "fit"), None, None, ("occ", "sub")),
        P(("grp", "fit"), None, None),
        P(("grp", "fit"), None),
    )
    return jax.shard_map(
        functools.partial(on_device, sizes),
        mesh=mesh,
        in_specs=placed,
        out_specs=P(("grp", "fit"), ("occ", "sub"), None),
        check_vma=False,
    )
```

```python
import functools

import jax
import jax.numpy as jnp
from jax import lax
from jax.experimental import pallas as pl
from jax.experimental.pallas import tpu as pltpu
from jax.sharding import PartitionSpec as P

BLK = 128
MESH = pl.DeviceIdType.MESH
OVER_ROWS = (((0,), (0,)), ((), ()))


def each(count, step):
    if count <= 16:
        for k in range(count):
            step(k)
    else:
        lax.fori_loop(0, count, lambda k, carry: (step(k), carry)[1], 0)


def kernel(
    sizes, owners_hbm, metric_hbm, tiles_hbm, out,
    owners, metric, tiles, acc, send1, recv1, send2, recv2,
    small_sem, load_sem, send1_sem, recv1_sem, send2_sem, recv2_sem,
):
    fit, occ, sub = sizes
    shards = occ * sub
    tile_rows, pairs, _, width = tiles.shape
    count, rows, _ = send1.shape
    my_fit, my_occ, my_sub = lax.axis_index("fit"), lax.axis_index("occ"), lax.axis_index("sub")

    if sub > 1:
        half = sub // 2
        own_class = lax.rem(my_sub, 2)
        my_slot = (my_fit * occ + my_occ) * half + my_sub // 2
        partner = {"fit": my_fit, "occ": my_occ, "sub": my_sub + 1 - 2 * own_class}

        def place(slot, kind):
            return slot // (occ * half), (slot // half) % occ, (slot % half) * 2 + kind
    else:
        own_class = lax.rem(my_fit, 2)
        my_slot = (my_fit // 2) * occ + my_occ
        partner = {"fit": my_fit + 1 - 2 * own_class, "occ": my_occ, "sub": my_sub}

        def place(slot, kind):
            return (slot // occ) * 2 + kind, slot % occ, 0

    def device_of(slot):
        owner, o, s = place(slot, own_class)
        return {"fit": owner, "occ": o, "sub": s}

    def partial(slot, kind):
        owner, o, s = place(slot, kind)
        return acc[owner, pl.ds(pl.multiple_of((o * sub + s) * rows, rows), rows), :]

    def other(k):
        return lax.rem(my_slot + k, count)

    def load(f, p):
        return pltpu.make_async_copy(tiles_hbm.at[f, p], tiles.at[f, p], load_sem.at[f, p])

    get_metric = pltpu.make_async_copy(metric_hbm, metric, small_sem.at[0])
    get_owners = pltpu.make_async_copy(owners_hbm, owners, small_sem.at[1])
    get_metric.start()
    get_owners.start()
    for f in range(tile_rows):
        for p in range(pairs):
            load(f, p).start()

    barrier = pltpu.get_barrier_semaphore()
    pl.semaphore_signal(barrier, inc=1, device_id=partner, device_id_type=MESH)
    each(count - 1, lambda k: pl.semaphore_signal(
        barrier, inc=1, device_id=device_of(other(k + 1)), device_id_type=MESH))

    acc[...] = jnp.zeros_like(acc)
    group = 2 if tile_rows % 2 == 0 else 1

    def work(step, carry, first=False):
        members = [step * group + g for g in range(group)]
        stacked = []
        if not first:
            for f in members:
                for p in range(pairs):
                    load(f, p).wait()
        for f in members:
            for p in range(pairs):
                if first:
                    load(f, p).wait()
                fitted = jnp.dot(
                    metric[f], tiles[f, p], preferred_element_type=jnp.float32
                ).astype(jnp.bfloat16)
                stacked.append(jnp.concatenate(
                    [fitted[:, c:c + BLK] for c in range(0, width, BLK)], axis=0))
        grams = [
            lax.dot_general(x, x, OVER_ROWS, preferred_element_type=jnp.float32) for x in stacked
        ]
        names = [owners[p, f] for f in members for p in range(pairs)]

        def add(d):
            total = acc[d]
            for name, gram in zip(names, grams):
                total = total + jnp.where(name == d, gram, 0.0)
            acc[d] = total

        for d in range(fit):
            add(d)
        return carry

    get_metric.wait()
    get_owners.wait()
    work(0, 0, first=True)
    lax.fori_loop(1, tile_rows // group, work, 0)

    pl.semaphore_wait(barrier, count)

    def swap(slot):
        return pltpu.make_async_remote_copy(
            src_ref=send1.at[slot], dst_ref=recv1.at[slot],
            send_sem=send1_sem.at[slot], recv_sem=recv1_sem.at[slot],
            device_id=partner, device_id_type=MESH)

    def deliver(slot):
        return pltpu.make_async_remote_copy(
            src_ref=send2.at[slot], dst_ref=recv2.at[my_slot],
            send_sem=send2_sem.at[slot], recv_sem=recv2_sem.at[my_slot],
            device_id=device_of(slot), device_id_type=MESH)

    def arrived(slot):
        return pltpu.make_async_remote_copy(
            src_ref=send2.at[slot], dst_ref=recv2.at[slot],
            send_sem=send2_sem.at[slot], recv_sem=recv2_sem.at[slot],
            device_id=device_of(slot), device_id_type=MESH)

    def give(k):
        slot = other(k + 1)
        send1[slot] = partial(slot, 1 - own_class).astype(jnp.bfloat16)
        swap(slot).start()

    each(count, give)

    def summed(slot):
        swap(slot).wait_recv()
        return partial(slot, own_class) + recv1[slot].astype(jnp.float32)

    def pass_on(k):
        slot = other(k + 1)
        send2[slot] = summed(slot).astype(jnp.bfloat16)
        deliver(slot).start()

    each(count - 1, pass_on)
    total = summed(my_slot)

    def collect(k, total):
        slot = other(count - 1 - k)
        arrived(slot).wait_recv()
        return total + recv2[slot].astype(jnp.float32)

    if count <= 16:
        for k in range(count - 1):
            total = collect(k, total)
    else:
        total = lax.fori_loop(0, count - 1, collect, total)
    out[0] = total.astype(out.dtype)

    each(count, lambda k: swap(other(k + 1)).wait_send())
    each(count - 1, lambda k: deliver(other(k + 1)).wait_send())


def on_device(sizes, tiles, metric, owners):
    fit, occ, sub = sizes
    count = fit * occ * sub // 2
    rows = BLK // (occ * sub)
    tile_rows, pairs, fit_rows, width = tiles.shape
    parts = pltpu.VMEM((count, rows, BLK), jnp.bfloat16)
    return pl.pallas_call(
        functools.partial(kernel, sizes),
        out_shape=pltpu.VMEM((1, rows, BLK), jnp.bfloat16),
        in_specs=[
            pl.BlockSpec(memory_space=pl.ANY),
            pl.BlockSpec(memory_space=pl.ANY),
            pl.BlockSpec(memory_space=pl.ANY),
        ],
        out_specs=pl.BlockSpec(memory_space=pltpu.VMEM),
        scratch_shapes=[
            pltpu.SMEM((pairs, tile_rows), jnp.int32),
            pltpu.VMEM(metric.shape, jnp.bfloat16),
            pltpu.VMEM(tiles.shape, jnp.bfloat16),
            pltpu.VMEM((fit, BLK, BLK), jnp.float32),
            parts, parts, parts, parts,
            pltpu.SemaphoreType.DMA((2,)),
            pltpu.SemaphoreType.DMA((tile_rows, pairs)),
            pltpu.SemaphoreType.DMA((count,)),
            pltpu.SemaphoreType.DMA((count,)),
            pltpu.SemaphoreType.DMA((count,)),
            pltpu.SemaphoreType.DMA((count,)),
        ],
        compiler_params=pltpu.CompilerParams(
            collective_id=0, has_side_effects=True, vmem_limit_bytes=56 << 20
        ),
    )(owners.T, metric, tiles)


def solution(mesh):
    sizes = tuple(mesh.shape[name] for name in ("fit", "occ", "sub"))
    placed = (
        P(("grp", "fit"), None, None, ("occ", "sub")),
        P(("grp", "fit"), None, None),
        P(("grp", "fit"), None),
    )
    return jax.shard_map(
        functools.partial(on_device, sizes),
        mesh=mesh,
        in_specs=placed,
        out_specs=P(("grp", "fit"), ("occ", "sub"), None),
        check_vma=False,
    )
```

```python
import functools

import jax
import jax.numpy as jnp
from jax import lax
from jax.experimental import pallas as pl
from jax.experimental.pallas import tpu as pltpu
from jax.sharding import PartitionSpec as P

BLK = 128
MESH = pl.DeviceIdType.MESH
OVER_ROWS = (((0,), (0,)), ((), ()))


def each(count, step):
    if count <= 16:
        for k in range(count):
            step(k)
    else:
        lax.fori_loop(0, count, lambda k, carry: (step(k), carry)[1], 0)


def kernel(
    sizes, owners, metric, tiles_hbm, out,
    tiles, acc, send1, recv1, send2, recv2,
    load_sem, send1_sem, recv1_sem, send2_sem, recv2_sem,
):
    fit, occ, sub = sizes
    shards = occ * sub
    tile_rows, pairs, _, width = tiles.shape
    count, rows, _ = send1.shape
    my_fit, my_occ, my_sub = lax.axis_index("fit"), lax.axis_index("occ"), lax.axis_index("sub")

    if sub > 1:
        half = sub // 2
        own_class = lax.rem(my_sub, 2)
        my_slot = (my_fit * occ + my_occ) * half + my_sub // 2
        partner = {"fit": my_fit, "occ": my_occ, "sub": my_sub + 1 - 2 * own_class}

        def place(slot, kind):
            return slot // (occ * half), (slot // half) % occ, (slot % half) * 2 + kind
    else:
        own_class = lax.rem(my_fit, 2)
        my_slot = (my_fit // 2) * occ + my_occ
        partner = {"fit": my_fit + 1 - 2 * own_class, "occ": my_occ, "sub": my_sub}

        def place(slot, kind):
            return (slot // occ) * 2 + kind, slot % occ, 0

    def device_of(slot):
        owner, o, s = place(slot, own_class)
        return {"fit": owner, "occ": o, "sub": s}

    def partial(slot, kind):
        owner, o, s = place(slot, kind)
        return acc[owner, pl.ds(pl.multiple_of((o * sub + s) * rows, rows), rows), :]

    def other(k):
        return lax.rem(my_slot + k, count)

    def load(f):
        return pltpu.make_async_copy(tiles_hbm.at[f], tiles.at[f], load_sem.at[f])

    for f in range(tile_rows):
        load(f).start()

    barrier = pltpu.get_barrier_semaphore()
    pl.semaphore_signal(barrier, inc=1, device_id=partner, device_id_type=MESH)
    each(count - 1, lambda k: pl.semaphore_signal(
        barrier, inc=1, device_id=device_of(other(k + 1)), device_id_type=MESH))

    acc[...] = jnp.zeros_like(acc)
    group = 2 if tile_rows % 2 == 0 else 1

    def work(step, carry):
        members = [step * group + g for g in range(group)]
        for f in members:
            load(f).wait()
        stacked = []
        for f in members:
            for p in range(pairs):
                fitted = jnp.dot(
                    metric[f], tiles[f, p], preferred_element_type=jnp.float32
                ).astype(jnp.bfloat16)
                stacked.append(jnp.concatenate(
                    [fitted[:, c:c + BLK] for c in range(0, width, BLK)], axis=0))
        grams = [
            lax.dot_general(x, x, OVER_ROWS, preferred_element_type=jnp.float32) for x in stacked
        ]
        names = [owners[p, f] for f in members for p in range(pairs)]

        def add(d):
            total = acc[d]
            for name, gram in zip(names, grams):
                total = total + jnp.where(name == d, gram, 0.0)
            acc[d] = total

        for d in range(fit):
            add(d)
        return carry

    lax.fori_loop(0, tile_rows // group, work, 0)

    pl.semaphore_wait(barrier, count)

    def swap(slot):
        return pltpu.make_async_remote_copy(
            src_ref=send1.at[slot], dst_ref=recv1.at[slot],
            send_sem=send1_sem.at[slot], recv_sem=recv1_sem.at[slot],
            device_id=partner, device_id_type=MESH)

    def deliver(slot):
        return pltpu.make_async_remote_copy(
            src_ref=send2.at[slot], dst_ref=recv2.at[my_slot],
            send_sem=send2_sem.at[slot], recv_sem=recv2_sem.at[my_slot],
            device_id=device_of(slot), device_id_type=MESH)

    def arrived(slot):
        return pltpu.make_async_remote_copy(
            src_ref=send2.at[slot], dst_ref=recv2.at[slot],
            send_sem=send2_sem.at[slot], recv_sem=recv2_sem.at[slot],
            device_id=device_of(slot), device_id_type=MESH)

    def give(k):
        slot = other(k + 1)
        send1[slot] = partial(slot, 1 - own_class).astype(jnp.bfloat16)
        swap(slot).start()

    each(count, give)

    def summed(slot):
        swap(slot).wait_recv()
        return partial(slot, own_class) + recv1[slot].astype(jnp.float32)

    def pass_on(k):
        slot = other(k + 1)
        send2[slot] = summed(slot).astype(jnp.bfloat16)
        deliver(slot).start()

    each(count - 1, pass_on)
    total = summed(my_slot)

    def collect(k, total):
        slot = other(count - 1 - k)
        arrived(slot).wait_recv()
        return total + recv2[slot].astype(jnp.float32)

    if count <= 16:
        for k in range(count - 1):
            total = collect(k, total)
    else:
        total = lax.fori_loop(0, count - 1, collect, total)
    out[0] = total.astype(out.dtype)

    each(count, lambda k: swap(other(k + 1)).wait_send())
    each(count - 1, lambda k: deliver(other(k + 1)).wait_send())


def on_device(sizes, tiles, metric, owners):
    fit, occ, sub = sizes
    count = fit * occ * sub // 2
    rows = BLK // (occ * sub)
    tile_rows, pairs, fit_rows, width = tiles.shape
    parts = pltpu.VMEM((count, rows, BLK), jnp.bfloat16)
    return pl.pallas_call(
        functools.partial(kernel, sizes),
        out_shape=pltpu.VMEM((1, rows, BLK), jnp.bfloat16),
        in_specs=[
            pl.BlockSpec(memory_space=pltpu.SMEM),
            pl.BlockSpec(memory_space=pltpu.VMEM),
            pl.BlockSpec(memory_space=pl.ANY),
        ],
        out_specs=pl.BlockSpec(memory_space=pltpu.VMEM),
        scratch_shapes=[
            pltpu.VMEM(tiles.shape, jnp.bfloat16),
            pltpu.VMEM((fit, BLK, BLK), jnp.float32),
            parts, parts, parts, parts,
            pltpu.SemaphoreType.DMA((tile_rows,)),
            pltpu.SemaphoreType.DMA((count,)),
            pltpu.SemaphoreType.DMA((count,)),
            pltpu.SemaphoreType.DMA((count,)),
            pltpu.SemaphoreType.DMA((count,)),
        ],
        compiler_params=pltpu.CompilerParams(
            collective_id=0, has_side_effects=True, vmem_limit_bytes=56 << 20
        ),
    )(owners.T, metric, tiles)


def solution(mesh):
    sizes = tuple(mesh.shape[name] for name in ("fit", "occ", "sub"))
    placed = (
        P(("grp", "fit"), None, None, ("occ", "sub")),
        P(("grp", "fit"), None, None),
        P(("grp", "fit"), None),
    )
    return jax.shard_map(
        functools.partial(on_device, sizes),
        mesh=mesh,
        in_specs=placed,
        out_specs=P(("grp", "fit"), ("occ", "sub"), None),
        check_vma=False,
    )
```
